256 devices in a mesh: seg: 2 (over core), row: 128 (over z, y, x).
Axes of the slice: x: 4, y: 4, z: 8, core: 2. Of those that a mesh axis runs over, the one named last changes fastest.
Arguments:
- site_tensors: bfloat16 [4, 128, 4, 384, 384], P('seg', 'row'), may hold values from -1.5 to 1.5, as said below
- block_counts: int32 [4, 128], replicated, may hold values from 1 to 3, 256 in all within a row
- gate_even: float32 [16, 16], replicated, may hold values from -0.4 to 1.4, as said below
- gate_odd: float32 [16, 16], replicated, may hold values from -0.4 to 1.4, as said below
Outputs:
- evolved: bfloat16 [4, 128, 4, 384, 384], P('seg', 'row')
The draws below stay inside these ranges and needn't reach their ends.
Inputs may be any that keep to these rules, and one draw needn't show every extreme that they name: block_counts[i, c] counts the live blocks of 128 rows of sector c on the bond left of site i; each row of block_counts sums to 256. `site_tensors`: entries in padded rows and columns are ignored. `gate_even`: only entries that conserve the charge are used. `gate_odd`: only entries that conserve the charge are used.
All inputs are finite; a program needn't handle non-finite values. Where the reference program divides by a largest or mean magnitude, that divisor is 1e-20 or more.
Results may differ from the reference program's by a relative error of at most 0.008.
Values may be sent and summed in bfloat16 or wider, within the bound.
A program may use at most 128 MiB of HBM per device.

```python
import math
import jax
import jax.numpy as jnp
import numpy as np
from jax import lax

BLOCK = 128
SLOTS = 3
PHYS = 4
SWEEPS = 6
SECTORS = 128
SITES = 4


def gate_with(noise):
    index = jnp.arange(PHYS * PHYS)
    return jnp.where(index[:, None] == index[None, :], 1.0 + noise, noise)


def draw_site_tensors(key, part):
    key = jax.random.fold_in(key, 11)
    off_key, diag_key = jax.random.split(key)
    row_count = SLOTS * BLOCK
    shape = (SITES, SECTORS, PHYS, row_count, row_count)
    sigma = 0.2 / math.sqrt(row_count)
    off_part = sigma * jax.random.truncated_normal(off_key, -4.0, 4.0, shape, jnp.float32)
    diag_part = jnp.exp(jax.random.uniform(diag_key, shape[:-1], jnp.float32, math.log(0.7), math.log(1.4)))
    index = jnp.arange(row_count)
    value = jnp.where(index[:, None] == index[None, :], diag_part[..., :, None], off_part)
    return value.astype(jnp.bfloat16)


def draw_gate_even(key, part):
    key = jax.random.fold_in(key, 21)
    noise = 0.12 * jax.random.truncated_normal(key, -3.0, 3.0, (PHYS * PHYS, PHYS * PHYS), jnp.float32)
    return gate_with(noise)


def draw_gate_odd(key, part):
    key = jax.random.fold_in(key, 22)
    noise = 0.12 * jax.random.truncated_normal(key, -3.0, 3.0, (PHYS * PHYS, PHYS * PHYS), jnp.float32)
    return gate_with(noise)


def split_up(amount, total, bound, skew):
    loads = [(1 << 20) // math.isqrt(rank ** skew) + 1 for rank in range(2, amount + 1)]
    spare, holding = total - bound - (amount - 1), [1] * (amount - 1)
    while spare > 0:
        candidates = [i for i in range(amount - 1) if holding[i] < bound]
        pool, remaining = sum([loads[i] for i in candidates]), spare
        for i in candidates:
            extra = min(bound - holding[i], max(1, remaining * loads[i] // pool), spare)
            holding[i] = holding[i] + extra
            spare = spare - extra
    return np.array([bound] + holding)


def uneven(rng, number_of, total, reach, slope):
    if number_of == 2:
        one = jax.random.randint(rng, (), max(1, total - reach), min(reach, total - 1) + 1)
        return jnp.stack([one, total - one])
    tallies = jnp.asarray(split_up(number_of, total, reach, slope), jnp.int32)
    twos = (number_of - 1) // 2
    source_of, receiver = tallies[1:1 + 2 * twos:2], tallies[2:2 + 2 * twos:2]
    slack = jnp.minimum(source_of - 1, reach - receiver)
    moved = jax.random.randint(jax.random.fold_in(rng, 1), (twos,), 0, 1 << 20) % (slack + 1)
    tallies = tallies.at[1:1 + 2 * twos:2].set(source_of - moved).at[2:2 + 2 * twos:2].set(receiver + moved)
    return tallies[jax.random.permutation(jax.random.fold_in(rng, 2), number_of)]


def setup_inputs(seed: int = 0) -> dict:
    key_list = jax.random.split(jax.random.key(seed), 5)
    site_tensors = draw_site_tensors(jax.random.fold_in(key_list[4], 71), 0)
    block_counts = jax.vmap(lambda own: uneven(own, SECTORS, 2 * SECTORS, SLOTS, 2))(jax.random.split(key_list[1], SITES)).reshape((SITES, SECTORS)).astype(jnp.int32)
    gate_even = draw_gate_even(jax.random.fold_in(key_list[4], 71), 0)
    gate_odd = draw_gate_odd(jax.random.fold_in(key_list[4], 71), 0)
    return {"site_tensors": site_tensors, "block_counts": block_counts, "gate_even": gate_even, "gate_odd": gate_odd}


CHARGE_SHIFT = (-1, 0, 0, 1)
HIGHEST = lax.Precision.HIGHEST

def neighbours(stack, offset):
    zero = jnp.zeros_like(stack[:1])
    padded = jnp.concatenate([zero, stack, zero], axis=0)
    return lax.slice_in_dim(padded, 1 + offset, 1 + offset + stack.shape[0], axis=0)

def conserving():
    charge = np.array(CHARGE_SHIFT)
    summed = (charge[:, None] + charge[None, :]).reshape(-1)
    return jnp.asarray((summed[:, None] == summed[None, :]).astype(np.float32))

def inverse_root(gram_matrix):
    row_count = gram_matrix.shape[-1]
    identity = jnp.eye(row_count, dtype=gram_matrix.dtype)
    widest = lax.optimization_barrier(jnp.max(lax.optimization_barrier(jnp.sum(jnp.abs(gram_matrix), axis=-1)), axis=-1))
    current = gram_matrix / widest[..., None, None]
    factor = jnp.broadcast_to(identity, gram_matrix.shape)
    for sweep in range(SWEEPS):
        step_matrix = 0.5 * (3.0 * identity - jnp.matmul(factor, current, precision=HIGHEST))
        current = jnp.matmul(current, step_matrix, precision=HIGHEST)
        factor = jnp.matmul(step_matrix, factor, precision=HIGHEST)
    return factor / jnp.sqrt(widest)[..., None, None]

def site_mask(tensor, left_counts, right_counts):
    sectors = tensor.shape[0]
    row_count = tensor.shape[-1]
    slot_index = jnp.arange(row_count, dtype=jnp.int32) // BLOCK
    row_live = slot_index[None, :] < left_counts[:, None]
    targets = jnp.arange(sectors, dtype=jnp.int32)[:, None] + jnp.array(CHARGE_SHIFT, jnp.int32)[None, :]
    onehot = targets[:, :, None] == jnp.arange(sectors, dtype=jnp.int32)[None, None, :]
    col_count = lax.optimization_barrier(jnp.sum(jnp.where(onehot, right_counts[None, None, :], 0), axis=2))
    col_live = slot_index[None, None, :] < col_count[:, :, None]
    keep = row_live[:, None, :, None] & col_live[:, :, None, :]
    return jnp.where(keep, tensor, jnp.zeros_like(tensor))

def bond_update(left_tensor, right_tensor, layer_gate, mid_counts):
    sectors = left_tensor.shape[0]
    row_count = left_tensor.shape[-1]
    gate_used = layer_gate * conserving()
    left32 = left_tensor.astype(jnp.float32)
    right32 = right_tensor.astype(jnp.float32)
    beside = jnp.stack([neighbours(right32, CHARGE_SHIFT[s]) for s in range(4)], axis=1)
    theta = jnp.einsum('csab,cstbd->cstad', left32, beside, precision=HIGHEST)
    mixed = jnp.einsum('kj,cjad->ckad', gate_used, theta.reshape(sectors, 16, row_count, row_count), precision=HIGHEST)
    mixed = mixed.astype(jnp.bfloat16).reshape(sectors, 4, 4, row_count, row_count)
    mixed32 = mixed.astype(jnp.float32)
    projected = jnp.einsum('ctuab,ctuxb->ctax', mixed32, beside, precision=HIGHEST)
    partial_grams = jnp.einsum('ctam,ctan->ctmn', projected, projected, precision=HIGHEST)
    slot_index = jnp.arange(row_count, dtype=jnp.int32) // BLOCK
    padding = (slot_index[None, :] >= mid_counts[:, None]).astype(jnp.float32)
    identity = jnp.eye(row_count, dtype=jnp.float32)
    gram_matrix = partial_grams[:, 1] + partial_grams[:, 2] + neighbours(partial_grams[:, 0], 1) + neighbours(partial_grams[:, 3], -1)
    gram_matrix = gram_matrix + padding[:, :, None] * identity
    inverse = inverse_root(gram_matrix)
    factor_beside = jnp.stack([neighbours(inverse, CHARGE_SHIFT[t]) for t in range(4)], axis=1)
    new_left = jnp.einsum('ctab,ctbd->ctad', projected, factor_beside, precision=HIGHEST).astype(jnp.bfloat16)
    right_terms = jnp.einsum('ctam,ctuab->ctumb', new_left.astype(jnp.float32), mixed32, precision=HIGHEST)
    right_terms = lax.optimization_barrier(right_terms.astype(jnp.bfloat16)).astype(jnp.float32)
    summed = right_terms[:, 1] + right_terms[:, 2] + neighbours(right_terms[:, 0], 1) + neighbours(right_terms[:, 3], -1)
    return (new_left, summed.astype(jnp.bfloat16))

def reference(site_tensors, block_counts, gate_even, gate_odd):
    site_count = site_tensors.shape[0]
    right_counts = jnp.roll(block_counts, -1, axis=0)
    chain_state = jax.vmap(site_mask)(site_tensors, block_counts, right_counts)
    for parity, layer_gate in ((0, gate_even), (1, gate_odd)):
        bond_count = (site_count - parity) // 2
        left_index = (parity + 2 * jnp.arange(bond_count, dtype=jnp.int32)).astype(jnp.int32)
        left_blocks = chain_state[left_index]
        right_blocks = chain_state[left_index + 1]
        mid_counts = block_counts[left_index + 1]
        new_lefts, new_rights = lax.map(lambda bundle: bond_update(bundle[0], bundle[1], layer_gate, bundle[2]), (left_blocks, right_blocks, mid_counts))
        chain_state = chain_state.at[left_index].set(new_lefts).at[left_index + 1].set(new_rights)
    return chain_state
```

```python
import functools

import jax
import jax.numpy as jnp
from jax import lax
from jax.experimental import pallas as pl
from jax.experimental.pallas import tpu as pltpu
from jax.sharding import PartitionSpec as P

MESH = pl.DeviceIdType.MESH
BF16, F32 = jnp.bfloat16, jnp.float32
BLOCK = 128
D = 384
SHIFT = (-1, 0, 0, 1)
ROWS = 16

MINUS = ((0, 1), (0, 2), (1, 0), (2, 0))
ZERO = ((0, 3), (1, 1), (1, 2), (2, 1), (2, 2), (3, 0))
PLUS = ((1, 3), (2, 3), (3, 1), (3, 2))


def dot(a, b):
    return jnp.dot(a, b, preferred_element_type=F32)


def dot_nt(a, b):
    return lax.dot_general(a, b, (((1,), (1,)), ((), ())), preferred_element_type=F32)


def split(x):
    high = x.astype(BF16)
    return high, (x - high.astype(F32)).astype(BF16)


def store_left(ref, x):
    high, low = split(x)
    ref[:, 0:D] = high
    ref[:, D : 2 * D] = low
    ref[:, 2 * D : 3 * D] = high


def store_right(ref, x, at):
    high, low = split(x)
    ref[0:D, at : at + D] = high
    ref[D : 2 * D, at : at + D] = high
    ref[2 * D : 3 * D, at : at + D] = low


def cols(s, count=1):
    return slice(s * D, (s + count) * D)


def kernel(x, counts, gate_even, gate_odd, out,
           left_m, right_m, halo_low, halo_high, edge_low, edge_high, send_0, send_3, mixed,
           returned, left_o, right_o, halo_low_o, halo_high_o, edge_low_o, edge_high_o,
           send_0o, send_3o, mixed_o, returned_o, right_new,
           theta_0, theta_12, theta_3, proj_r, new_t, new_l, new_lo, ns_s, ns_l, ns_g, ns_r, ns_q,
           send_sem, recv_sem):
    seg, row = lax.axis_index("seg"), lax.axis_index("row")
    rows = lax.axis_size("row")
    up, down = lax.rem(row + 1, rows), lax.rem(row + rows - 1, rows)
    first, last = row == 0, row == rows - 1

    barrier = pltpu.get_barrier_semaphore()
    for target in ((seg, up), (seg, down), (1 - seg, row), (1 - seg, up), (1 - seg, down)):
        pl.semaphore_signal(barrier, inc=1, device_id=target, device_id_type=MESH)

    def copy(k, src, dst, target):
        return pltpu.make_async_remote_copy(
            src_ref=src, dst_ref=dst, send_sem=send_sem.at[k], recv_sem=recv_sem.at[k],
            device_id=target, device_id_type=MESH,
        )

    def live(site, sector, block):
        inside = (sector >= 0) & (sector < rows)
        count = counts[site, jnp.clip(sector, 0, rows - 1)]
        return jnp.where(inside & (block < count), 1.0, 0.0).astype(F32)

    def mask(slot, store):
        site = 2 * seg + slot
        right_site = lax.rem(site + 1, 4)
        row_live = [live(site, row, i) for i in range(3)]
        for s in (1, 2, 0, 3):
            col_live = [live(right_site, row + SHIFT[s], j) for j in range(3)]
            for i in range(3):
                for j in range(3):
                    r0, c0 = s * D + i * BLOCK, j * BLOCK
                    block = x[slot, r0 : r0 + BLOCK, c0 : c0 + BLOCK].astype(F32)
                    store(s, i * BLOCK, c0, (block * (row_live[i] * col_live[j])).astype(BF16))

    def store_r(s, r0, c0, block):
        right_m[r0 : r0 + BLOCK, s * D + c0 : s * D + c0 + BLOCK] = block

    def store_l(s, r0, c0, block):
        left_m[s * D + r0 : s * D + r0 + BLOCK, c0 : c0 + BLOCK] = block

    mask(1, store_r)
    pl.semaphore_wait(barrier, 5)

    even_r = [
        copy(0, right_m.at[:, cols(1, 2)], halo_low.at[:, cols(0, 2)], (seg, up)),
        copy(1, right_m.at[:, cols(1, 2)], halo_high.at[:, cols(1, 2)], (seg, down)),
        copy(2, right_m.at[:, cols(3)], halo_low.at[:, cols(2)], (seg, up)),
        copy(3, right_m.at[:, cols(0)], halo_high.at[:, cols(0)], (seg, down)),
    ]
    for c in even_r:
        c.start()
    mask(0, store_l)

    def edge_copies(base, left, low, high):
        return [
            copy(base, left.at[3 * D : 4 * D, :], low, (seg, up)),
            copy(base + 1, left.at[0:D, :], high, (seg, down)),
        ]

    def mixed_copies(base, s0, s3, x_ref):
        return [
            copy(base, s0.at[:, cols(0, 2)], x_ref.at[0:D, cols(1, 2)], (seg, down)),
            copy(base + 1, s3.at[:, cols(1, 2)], x_ref.at[3 * D : 4 * D, cols(1, 2)], (seg, up)),
            copy(base + 2, s0.at[:, cols(2)], x_ref.at[0:D, cols(3)], (seg, down)),
            copy(base + 3, s3.at[:, cols(0)], x_ref.at[3 * D : 4 * D, cols(0)], (seg, up)),
        ]

    def zero(ref, where):
        @pl.when(where)
        def _():
            ref[...] = jnp.zeros(ref.shape, ref.dtype)

    def mix(gate, pairs, s0, s3, x_ref):
        def source(s1, s2, r):
            if s1 == 0:
                return theta_0[pl.ds(r, ROWS), cols(s2 - 1)]
            if s1 == 3:
                return theta_3[pl.ds(r, ROWS), cols(s2)]
            return theta_12[pl.ds(r + (s1 - 1) * D, ROWS), cols(s2)]

        def step(i, carry):
            r = pl.multiple_of(i * ROWS, ROWS)
            parts = [source(s1, s2, r) for s1, s2 in pairs]
            for t1, t2 in pairs:
                total = None
                for (s1, s2), part in zip(pairs, parts):
                    term = gate[4 * t1 + t2, 4 * s1 + s2] * part
                    total = term if total is None else total + term
                total = total.astype(BF16)
                if t1 == 0:
                    s0[pl.ds(r, ROWS), cols(t2 - 1)] = total
                elif t1 == 3:
                    s3[pl.ds(r, ROWS), cols(t2)] = total
                else:
                    x_ref[pl.ds(r + t1 * D, ROWS), cols(t2)] = total
            return carry

        lax.fori_loop(0, D // ROWS, step, 0)

    def project(right, x_ref, t, count):
        value = dot_nt(right[...], x_ref[t * D : (t + count) * D, :])
        high, low = split(value)
        proj_r[0:D, cols(t, count)] = high
        proj_r[D : 2 * D, cols(t, count)] = high
        proj_r[2 * D : 3 * D, cols(t, count)] = low

    def inverse_root(mid_site):
        both = dot_nt(proj_r[0:D, :], proj_r[D : 3 * D, :])
        cross = both[:, D : 2 * D]
        gram = both[:, 0:D] + cross + cross.T
        i0 = lax.broadcasted_iota(jnp.int32, (D, D), 0)
        i1 = lax.broadcasted_iota(jnp.int32, (D, D), 1)
        identity = jnp.where(i0 == i1, 1.0, 0.0).astype(F32)
        live_rows = counts[mid_site, row] * BLOCK
        gram = gram + jnp.where((i0 == i1) & (i0 >= live_rows), 1.0, 0.0)
        widest = jnp.max(jnp.sum(jnp.abs(gram), axis=0, keepdims=True), axis=1, keepdims=True)
        ns_s[...] = gram / widest
        for pair in range(3):
            s = ns_s[...]
            store_left(ns_l, s)
            store_right(ns_r, s, 0)
            square = dot(ns_l[...], ns_r[:, 0:D])
            store_right(ns_q, (square - 9.0 * s + 27.0 * identity) * 0.0625, 0)
            store_left(ns_l, square)
            growth = dot(ns_l[...], ns_q[...]) + (36.0 * identity - 39.0 * s) * 0.0625
            store_left(ns_g, growth)
            if pair == 0:
                factor = growth
                moved = dot(ns_g[...], ns_r[:, 0:D])
            elif pair == 1:
                product = dot(ns_g[...], ns_r[...])
                moved, factor = product[:, 0:D], product[:, D : 2 * D]
            else:
                factor = dot(ns_g[...], ns_r[:, D : 2 * D])
            if pair < 2:
                store_right(ns_r, factor, D)
                store_right(ns_q, moved, 0)
                ns_s[...] = dot(ns_g[...], ns_q[...])
        store_left(ns_l, factor / jnp.sqrt(widest))
        new_t[...] = dot(ns_l[...], proj_r[...]).astype(BF16)

    def new_left(dst):
        i0 = lax.broadcasted_iota(jnp.int32, (D, D), 0)
        i1 = lax.broadcasted_iota(jnp.int32, (D, D), 1)
        identity = jnp.where(i0 == i1, 1.0, 0.0).astype(BF16)
        for t in (0, 3, 1, 2):
            dst[t * D : (t + 1) * D, :] = dot_nt(identity, new_t[:, cols(t)]).astype(BF16)

    def new_right(x_ref, store):
        for half in range(2):
            value = dot(new_t[...], x_ref[:, cols(2 * half, 2)]).astype(BF16)
            store(2 * half, value[:, 0:D])
            store(2 * half + 1, value[:, D : 2 * D])

    def bond(gate, mid_site, left, right, low, high, arrivals, edges, sends, e_low, e_high,
             s0, s3, x_ref):
        theta_12[...] = dot(left[D : 3 * D, :], right[...])
        arrivals[0]()
        theta_0[:, cols(0, 2)] = dot(left[0:D, :], low[:, cols(0, 2)])
        arrivals[1]()
        theta_3[:, cols(1, 2)] = dot(left[3 * D : 4 * D, :], high[:, cols(1, 2)])
        mix(gate, MINUS, s0, s3, x_ref)
        sends[0].start()
        mix(gate, PLUS, s0, s3, x_ref)
        sends[1].start()
        arrivals[2]()
        theta_0[:, cols(2)] = dot(left[0:D, :], low[:, cols(2)])
        arrivals[3]()
        theta_3[:, cols(0)] = dot(left[3 * D : 4 * D, :], high[:, cols(0)])
        mix(gate, ZERO, s0, s3, x_ref)
        sends[2].start()
        sends[3].start()
        project(right, x_ref, 1, 2)
        for c in edges:
            c.wait_recv()
        x_ref[0:D, cols(0)] = (gate[0, 0] * dot(e_high[...], right[:, cols(0)])).astype(BF16)
        x_ref[3 * D : 4 * D, cols(3)] = (gate[15, 15] * dot(e_low[...], right[:, cols(3)])).astype(BF16)
        for c in sends:
            c.wait_recv()
        zero(x_ref.at[0:D, :], last)
        zero(x_ref.at[3 * D : 4 * D, :], first)
        project(right, x_ref, 0, 1)
        project(right, x_ref, 3, 1)
        inverse_root(mid_site)

    edges = edge_copies(4, left_m, edge_low, edge_high)
    for c in edges:
        c.start()
    sends = mixed_copies(6, send_0, send_3, mixed)

    def arrive(k, ref, where):
        def wait():
            even_r[k].wait_recv()
            zero(ref, where)
        return wait

    bond(gate_even, 2 * seg + 1, left_m, right_m, halo_low, halo_high,
         [arrive(0, halo_low.at[:, cols(0, 2)], first), arrive(1, halo_high.at[:, cols(1, 2)], last),
          arrive(2, halo_low.at[:, cols(2)], first), arrive(3, halo_high.at[:, cols(0)], last)],
         edges, sends, edge_low, edge_high, send_0, send_3, mixed)

    new_left(new_l)
    back = [
        copy(10, new_l.at[0:D, :], returned.at[0:D, :], (0, up)),
        copy(11, new_l.at[3 * D : 4 * D, :], returned.at[D : 2 * D, :], (0, down)),
    ]
    move = [
        copy(12, new_l.at[D : 2 * D, :], halo_low_o.at[:, cols(0)], (0, up)),
        copy(13, new_l.at[D : 2 * D, :], halo_high_o.at[:, cols(1)], (0, down)),
        copy(14, new_l.at[2 * D : 3 * D, :], halo_low_o.at[:, cols(1)], (0, up)),
        copy(15, new_l.at[2 * D : 3 * D, :], halo_high_o.at[:, cols(2)], (0, down)),
        copy(16, new_l.at[0:D, :], right_o.at[:, cols(0)], (0, up)),
        copy(17, new_l.at[3 * D : 4 * D, :], right_o.at[:, cols(3)], (0, down)),
        copy(18, new_l.at[D : 2 * D, :], right_o.at[:, cols(1)], (0, row)),
        copy(19, new_l.at[2 * D : 3 * D, :], right_o.at[:, cols(2)], (0, row)),
        copy(20, new_l.at[3 * D : 4 * D, :], halo_low_o.at[:, cols(2)], (0, row)),
        copy(21, new_l.at[0:D, :], halo_high_o.at[:, cols(0)], (0, row)),
    ]
    odd_edges = edge_copies(22, left_o, edge_low_o, edge_high_o)
    odd_sends = mixed_copies(24, send_0o, send_3o, mixed_o)
    odd_back = [
        copy(28, new_lo.at[0:D, :], returned_o.at[0:D, :], (0, up)),
        copy(29, new_lo.at[3 * D : 4 * D, :], returned_o.at[D : 2 * D, :], (0, down)),
    ]
    hand_over = copy(30, left_m, right_new, (1, row))

    @pl.when(seg == 1)
    def _():
        for c in move:
            c.start()

        def store(s, value):
            out[1, s * D : (s + 1) * D, :] = value

        new_right(mixed, store)
        for c in move:
            c.wait_send()
        hand_over.wait_recv()
        out[0, :, :] = right_new[...]

    @pl.when(seg == 0)
    def _():
        for c in back:
            c.start()

        def store(s, value):
            left_o[s * D : (s + 1) * D, :] = value

        new_right(mixed, store)
        for c in odd_edges:
            c.start()
        out[0, D : 3 * D, :] = new_l[D : 3 * D, :]

        def arrive_own():
            for k in (4, 5, 6, 7):
                move[k].wait_recv()
            zero(right_o.at[:, cols(0)], first)
            zero(right_o.at[:, cols(3)], last)

        def arrive_low():
            move[0].wait_recv()
            move[2].wait_recv()
            zero(halo_low_o.at[:, cols(0, 2)], first)

        def arrive_high():
            move[1].wait_recv()
            move[3].wait_recv()
            zero(halo_high_o.at[:, cols(1, 2)], last)

        def arrive_low_3():
            move[8].wait_recv()
            zero(halo_low_o.at[:, cols(2)], first)

        def arrive_high_0():
            move[9].wait_recv()
            zero(halo_high_o.at[:, cols(0)], last)

        arrive_own()
        bond(gate_odd, 2, left_o, right_o, halo_low_o, halo_high_o,
             [arrive_low, arrive_high, arrive_low_3, arrive_high_0],
             odd_edges, odd_sends, edge_low_o, edge_high_o, send_0o, send_3o, mixed_o)
        new_left(new_lo)
        for c in odd_back:
            c.start()
        for c in edges:
            c.wait_send()

        def store_new(s, value):
            left_m[s * D : (s + 1) * D, :] = value

        new_right(mixed_o, store_new)
        hand_over.start()
        out[1, D : 3 * D, :] = new_lo[D : 3 * D, :]
        for source, slot, copies in ((returned, 0, back), (returned_o, 1, odd_back)):
            for c in copies:
                c.wait_recv()
            zero(source.at[0:D, :], first)
            zero(source.at[D : 2 * D, :], last)
            out[slot, 0:D, :] = source[0:D, :]
            out[slot, 3 * D : 4 * D, :] = source[D : 2 * D, :]
        for c in back + odd_edges + odd_sends + odd_back + [hand_over]:
            c.wait_send()

    @pl.when(seg == 1)
    def _():
        for c in edges:
            c.wait_send()

    for c in even_r + sends:
        c.wait_send()


def body(site_tensors, block_counts, gate_even, gate_odd):
    sites = site_tensors.shape[0]
    x = site_tensors.reshape(sites, 4 * D, D)
    vmem = pl.BlockSpec(memory_space=pltpu.VMEM)
    smem = pl.BlockSpec(memory_space=pltpu.SMEM)
    unit = lambda r, c, dtype=BF16: pltpu.VMEM((r * D, c * D), dtype)
    phase = [unit(4, 1), unit(1, 4), unit(1, 3), unit(1, 3), unit(1, 1), unit(1, 1),
             unit(1, 3), unit(1, 3), unit(4, 4), unit(2, 1)]
    evolved = pl.pallas_call(
        kernel,
        out_shape=jax.ShapeDtypeStruct(x.shape, x.dtype),
        in_specs=[vmem, smem, smem, smem],
        out_specs=vmem,
        scratch_shapes=phase + phase + [
            unit(4, 1),
            unit(1, 3, F32), unit(2, 4, F32), unit(1, 3, F32),
            unit(3, 4), unit(1, 4), unit(4, 1), unit(4, 1),
            unit(1, 1, F32), unit(1, 3), unit(1, 3), unit(3, 2), unit(3, 1),
            pltpu.SemaphoreType.DMA((31,)), pltpu.SemaphoreType.DMA((31,)),
        ],
        compiler_params=pltpu.CompilerParams(
            collective_id=0, has_side_effects=True, vmem_limit_bytes=60 * 2**20
        ),
    )(x, block_counts, gate_even, gate_odd)
    return evolved.reshape(site_tensors.shape)


def solution(mesh):
    in_specs = (P("seg", "row", None, None, None), P(), P(), P())
    out_specs = P("seg", "row", None, None, None)
    return jax.shard_map(body, mesh=mesh, in_specs=in_specs, out_specs=out_specs, check_vma=False)
```

```python
import functools

import jax
import jax.numpy as jnp
from jax import lax
from jax.experimental import pallas as pl
from jax.experimental.pallas import tpu as pltpu
from jax.sharding import PartitionSpec as P

MESH = pl.DeviceIdType.MESH
BF16, F32 = jnp.bfloat16, jnp.float32
BLOCK = 128
D = 384
SHIFT = (-1, 0, 0, 1)
ROWS = 16

MINUS = ((0, 1), (0, 2), (1, 0), (2, 0))
ZERO = ((0, 3), (1, 1), (1, 2), (2, 1), (2, 2), (3, 0))
PLUS = ((1, 3), (2, 3), (3, 1), (3, 2))


def dot(a, b):
    return jnp.dot(a, b, preferred_element_type=F32)


def dot_nt(a, b):
    return lax.dot_general(a, b, (((1,), (1,)), ((), ())), preferred_element_type=F32)


def split(x):
    high = x.astype(BF16)
    return high, (x - high.astype(F32)).astype(BF16)


def put(ref, x, at=0):
    high, low = split(x)
    ref[0, :, at : at + D] = high
    ref[1, :, at : at + D] = low


def dot3(a, b, start=0, stop=D):
    first, second = a[0, :, 0:D], a[1, :, 0:D]
    left = jnp.concatenate([first, first, second], axis=1)
    high, low = b[0, :, start:stop], b[1, :, start:stop]
    return dot(left, jnp.concatenate([high, low, high], axis=0))


def cols(s, count=1):
    return slice(s * D, (s + count) * D)


PLACE = (2, 0, 1, 3)


def at(t):
    return cols(PLACE[t])


def eye(dtype=F32):
    i0 = lax.broadcasted_iota(jnp.int32, (D, D), 0)
    i1 = lax.broadcasted_iota(jnp.int32, (D, D), 1)
    return jnp.where(i0 == i1, 1.0, 0.0).astype(dtype)


def kernel(x, counts, gate_even, gate_odd, out,
           right_m, halo_low, halo_high, edge_low, edge_high, send_0, send_3, mixed,
           right_o, halo_low_o, halo_high_o, edge_low_o, edge_high_o, send_0o, send_3o, mixed_o,
           x_v, left_m, left_o, new_r, theta_0, theta_12, theta_3, proj_r, new_t, new_l, new_lo,
           ns_rz, ns_q, ns_p, ns_g, send_sem, recv_sem, local_sem, go_sem):
    seg, row = lax.axis_index("seg"), lax.axis_index("row")
    rows = lax.axis_size("row")
    up, down = lax.rem(row + 1, rows), lax.rem(row + rows - 1, rows)

    loads = [pltpu.make_async_copy(x.at[k], x_v.at[k], local_sem.at[k]) for k in (0, 1)]
    loads[1].start()
    loads[0].start()
    barrier = pltpu.get_barrier_semaphore()
    for target in ((seg, up), (seg, down), (1 - seg, row), (1 - seg, up), (1 - seg, down)):
        pl.semaphore_signal(barrier, inc=1, device_id=target, device_id_type=MESH)

    def copy(k, src, dst, target):
        return pltpu.make_async_remote_copy(
            src_ref=src, dst_ref=dst, send_sem=send_sem.at[k], recv_sem=recv_sem.at[k],
            device_id=target, device_id_type=MESH,
        )

    def live(site, sector, block):
        inside = (sector >= 0) & (sector < rows)
        count = counts[site, jnp.clip(sector, 0, rows - 1)]
        return jnp.where(inside & (block < count), 1.0, 0.0).astype(F32)

    def mask(slot, store):
        site = 2 * seg + slot
        right_site = lax.rem(site + 1, 4)
        row_live = [live(site, row, i) for i in range(3)]
        for s in range(4):
            col_live = [live(right_site, row + SHIFT[s], j) for j in range(3)]
            for i in range(3):
                for j in range(3):
                    r0, c0 = s * D + i * BLOCK, j * BLOCK
                    block = x_v[slot, r0 : r0 + BLOCK, c0 : c0 + BLOCK].astype(F32)
                    store(s, i * BLOCK, c0, (block * (row_live[i] * col_live[j])).astype(BF16))

    def store_r(s, r0, c0, block):
        right_m[r0 : r0 + BLOCK, s * D + c0 : s * D + c0 + BLOCK] = block

    def store_l(s, r0, c0, block):
        left_m[s * D + r0 : s * D + r0 + BLOCK, c0 : c0 + BLOCK] = block

    def edge_copies(base, left, low, high):
        return [
            copy(base, left.at[3 * D : 4 * D, :], low, (seg, up)),
            copy(base + 1, left.at[0:D, :], high, (seg, down)),
        ]

    def mixed_copies(base, s0, s3, x_ref):
        return [
            copy(base, s0.at[:, cols(0, 2)], x_ref.at[at(0), cols(1, 2)], (seg, down)),
            copy(base + 1, s3.at[:, cols(1, 2)], x_ref.at[at(3), cols(1, 2)], (seg, up)),
            copy(base + 2, s0.at[:, cols(2)], x_ref.at[at(0), cols(3)], (seg, down)),
            copy(base + 3, s3.at[:, cols(0)], x_ref.at[at(3), cols(0)], (seg, up)),
        ]

    def mix(gate, pairs, right_site, s0, s3, x_ref):
        charge = SHIFT[pairs[0][0]] + SHIFT[pairs[0][1]]
        lane = lax.broadcasted_iota(jnp.int32, (ROWS, D), 1)
        count = counts[right_site, jnp.clip(row + charge, 0, rows - 1)]
        inside = (row + charge >= 0) & (row + charge < rows)
        keep = jnp.where(lane < jnp.where(inside, count, 0) * BLOCK, 1.0, 0.0).astype(F32)
        keep_0 = keep * jnp.where(row > 0, 1.0, 0.0).astype(F32)
        keep_3 = keep * jnp.where(row < rows - 1, 1.0, 0.0).astype(F32)

        def source(s1, s2, r):
            if s1 == 0:
                return theta_0[pl.ds(r, ROWS), cols(s2 - 1)]
            if s1 == 3:
                return theta_3[pl.ds(r, ROWS), cols(s2)]
            return theta_12[pl.ds(r + (s1 - 1) * D, ROWS), cols(s2)]

        def step(i, carry):
            r = pl.multiple_of(i * ROWS, ROWS)
            parts = [source(s1, s2, r) for s1, s2 in pairs]
            for t1, t2 in pairs:
                total = None
                for (s1, s2), part in zip(pairs, parts):
                    term = gate[4 * t1 + t2, 4 * s1 + s2] * part
                    total = term if total is None else total + term
                if t1 == 0:
                    s0[pl.ds(r, ROWS), cols(t2 - 1)] = (total * keep_0).astype(BF16)
                elif t1 == 3:
                    s3[pl.ds(r, ROWS), cols(t2)] = (total * keep_3).astype(BF16)
                else:
                    x_ref[pl.ds(r + PLACE[t1] * D, ROWS), cols(t2)] = (total * keep).astype(BF16)
            return carry

        lax.fori_loop(0, D // ROWS, step, 0)

    def store_projected(value, where):
        high, low = split(value)
        proj_r[0:D, where] = high
        proj_r[D : 2 * D, where] = high
        proj_r[2 * D : 3 * D, where] = low

    def gram_part(where):
        return dot_nt(proj_r[0:D, where], proj_r[D : 3 * D, where])

    def inverse_root(both, mid_site):
        identity = eye()
        cross = both[:, D : 2 * D]
        gram = both[:, 0:D] + cross + cross.T
        i0 = lax.broadcasted_iota(jnp.int32, (D, D), 0)
        gram = gram + jnp.where(i0 >= counts[mid_site, row] * BLOCK, identity, 0.0)
        widest = jnp.max(jnp.sum(jnp.abs(gram), axis=0, keepdims=True), axis=1, keepdims=True)
        s = gram / widest
        for pair in range(3):
            put(ns_rz, s)
            square = dot3(ns_rz, ns_rz)
            put(ns_q, (square - 9.0 * s + 27.0 * identity) * 0.0625)
            put(ns_p, square)
            growth = dot3(ns_p, ns_q) + (36.0 * identity - 39.0 * s) * 0.0625
            put(ns_g, growth)
            if pair == 0:
                factor, moved = growth, dot3(ns_g, ns_rz)
            elif pair == 1:
                product = dot3(ns_g, ns_rz, 0, 2 * D)
                moved, factor = product[:, 0:D], product[:, D : 2 * D]
            else:
                factor = dot3(ns_g, ns_rz, D, 2 * D)
            if pair < 2:
                put(ns_rz, factor, D)
                put(ns_q, moved)
                s = dot3(ns_g, ns_q)
        high, low = split(factor / jnp.sqrt(widest))
        left = jnp.concatenate([high, low, high], axis=1)
        new_t[...] = dot(left, proj_r[...]).astype(BF16)

    def new_left(dst, order):
        identity = eye(BF16)
        for t in order:
            dst[cols(t), :] = dot_nt(identity, new_t[:, at(t)]).astype(BF16)

    def new_right(x_ref, dst):
        for half in range(2):
            value = dot(new_t[...], x_ref[:, cols(2 * half, 2)]).astype(BF16)
            dst[cols(2 * half), :] = value[:, 0:D]
            dst[cols(2 * half + 1), :] = value[:, D : 2 * D]

    def bond(gate, mid_site, right_site, left, right, low, high, arrivals, edges, sends,
             e_low, e_high, s0, s3, x_ref, before_root):
        theta_12[:, cols(0)] = dot(left[cols(1, 2), :], right[:, cols(0)])
        arrivals[0]()
        theta_0[:, cols(0, 2)] = dot(left[cols(0), :], low[:, cols(0, 2)])
        mix(gate, MINUS, right_site, s0, s3, x_ref)
        sends[0].start()
        theta_12[:, cols(3)] = dot(left[cols(1, 2), :], right[:, cols(3)])
        arrivals[1]()
        theta_3[:, cols(1, 2)] = dot(left[cols(3), :], high[:, cols(1, 2)])
        mix(gate, PLUS, right_site, s0, s3, x_ref)
        sends[1].start()
        theta_12[:, cols(1, 2)] = dot(left[cols(1, 2), :], right[:, cols(1, 2)])
        arrivals[2]()
        theta_0[:, cols(2)] = dot(left[cols(0), :], low[:, cols(2)])
        arrivals[3]()
        theta_3[:, cols(0)] = dot(left[cols(3), :], high[:, cols(0)])
        mix(gate, ZERO, right_site, s0, s3, x_ref)
        sends[2].start()
        sends[3].start()
        inner, outer = cols(0, 2), cols(2, 2)
        store_projected(dot_nt(right[...], x_ref[inner, :]), inner)
        theta_12[0:D, cols(0, 2)] = gram_part(inner)
        for c in edges:
            c.wait_recv()
        x_ref[at(0), cols(0)] = (gate[0, 0] * dot(e_high[...], right[:, cols(0)])).astype(BF16)
        x_ref[at(3), cols(3)] = (gate[15, 15] * dot(e_low[...], right[:, cols(3)])).astype(BF16)
        for c in sends[:2]:
            c.wait_recv()
        theta_0[:, cols(0)] = dot_nt(right[:, cols(0, 3)], x_ref[at(0), cols(0, 3)])
        theta_3[:, cols(0)] = dot_nt(right[:, cols(1, 3)], x_ref[at(3), cols(1, 3)])
        sends[2].wait_recv()
        last_0 = dot_nt(right[:, cols(3)], x_ref[at(0), cols(3)])
        store_projected(theta_0[:, cols(0)] + last_0, at(0))
        sends[3].wait_recv()
        last_3 = dot_nt(right[:, cols(0)], x_ref[at(3), cols(0)])
        store_projected(theta_3[:, cols(0)] + last_3, at(3))
        before_root()
        inverse_root(theta_12[0:D, cols(0, 2)] + gram_part(outer), mid_site)

    xs = [x.at[1, cols(s), :] for s in range(4)]
    even_r = [
        copy(0, xs[1], halo_low.at[:, cols(0)], (seg, up)),
        copy(1, xs[2], halo_low.at[:, cols(1)], (seg, up)),
        copy(2, xs[1], halo_high.at[:, cols(1)], (seg, down)),
        copy(3, xs[2], halo_high.at[:, cols(2)], (seg, down)),
        copy(4, xs[3], halo_low.at[:, cols(2)], (seg, up)),
        copy(5, xs[0], halo_high.at[:, cols(0)], (seg, down)),
    ]
    edges = edge_copies(6, left_m, edge_low, edge_high)
    sends = mixed_copies(8, send_0, send_3, mixed)

    def start_even():
        for k in (0, 2, 1, 3, 4, 5):
            even_r[k].start()

    def arrive(*which):
        def wait():
            for k in which:
                even_r[k].wait_recv()
        return wait

    def wait_both(k):
        def wait():
            even_r[k].wait_recv()
            @pl.when(seg == 1)
            def _():
                pl.semaphore_signal(go_sem, inc=1, device_id=(0, row), device_id_type=MESH)
        return wait

    pl.semaphore_wait(barrier, 5)

    @pl.when(seg == 1)
    def _():
        start_even()

    loads[1].wait()
    mask(1, store_r)
    loads[0].wait()
    mask(0, store_l)

    @pl.when(seg == 0)
    def _():
        pl.semaphore_wait(go_sem, 1)
        start_even()

    for c in edges:
        c.start()
    bond(gate_even, 2 * seg + 1, lax.rem(2 * seg + 2, 4), left_m, right_m, halo_low, halo_high,
         [arrive(0, 1), arrive(2, 3), arrive(4), wait_both(5)], edges, sends,
         edge_low, edge_high, send_0, send_3, mixed, lambda: None)

    back = [
        copy(12, new_l.at[cols(0), :], out.at[0, cols(0), :], (0, up)),
        copy(13, new_l.at[cols(3), :], out.at[0, cols(3), :], (0, down)),
    ]
    move = [
        copy(14, new_l.at[cols(1), :], halo_low_o.at[:, cols(0)], (0, up)),
        copy(15, new_l.at[cols(2), :], halo_low_o.at[:, cols(1)], (0, up)),
        copy(16, new_l.at[cols(1), :], halo_high_o.at[:, cols(1)], (0, down)),
        copy(17, new_l.at[cols(2), :], halo_high_o.at[:, cols(2)], (0, down)),
        copy(18, new_l.at[cols(0), :], right_o.at[:, cols(0)], (0, up)),
        copy(19, new_l.at[cols(3), :], right_o.at[:, cols(3)], (0, down)),
        copy(20, new_l.at[cols(1), :], right_o.at[:, cols(1)], (0, row)),
        copy(21, new_l.at[cols(2), :], right_o.at[:, cols(2)], (0, row)),
        copy(22, new_l.at[cols(3), :], halo_low_o.at[:, cols(2)], (0, row)),
        copy(23, new_l.at[cols(0), :], halo_high_o.at[:, cols(0)], (0, row)),
    ]
    odd_edges = edge_copies(24, left_o, edge_low_o, edge_high_o)
    odd_sends = mixed_copies(26, send_0o, send_3o, mixed_o)
    odd_back = [
        copy(30, new_lo.at[cols(0), :], out.at[1, cols(0), :], (0, up)),
        copy(31, new_lo.at[cols(3), :], out.at[1, cols(3), :], (0, down)),
    ]
    hand_over = [
        copy(32 + h, new_r.at[cols(2 * h, 2), :], out.at[0, cols(2 * h, 2), :], (1, row))
        for h in range(2)
    ]

    @pl.when(seg == 1)
    def _():
        new_left(new_l, (0, 3, 1, 2))
        for k in (4, 5, 0, 2, 1, 3, 6, 7, 8, 9):
            move[k].start()
        new_right(mixed, new_r)
        keep = pltpu.make_async_copy(new_r, out.at[1], local_sem.at[2])
        keep.start()
        for c in hand_over:
            c.wait_recv()
        for c in move:
            c.wait_send()
        keep.wait()

    @pl.when(seg == 0)
    def _():
        new_right(mixed, left_o)
        for c in odd_edges:
            c.start()
        new_left(new_l, (0, 3, 1, 2))
        keep = pltpu.make_async_copy(new_l.at[cols(1, 2), :], out.at[0, cols(1, 2), :], local_sem.at[2])
        keep.start()

        def arrive_odd(*which):
            def wait():
                for k in which:
                    move[k].wait_recv()
            return wait

        def start_back():
            for c in back:
                c.start()

        arrive_odd(4, 5, 6, 7)()
        bond(gate_odd, 2, 3, left_o, right_o, halo_low_o, halo_high_o,
             [arrive_odd(0, 1), arrive_odd(2, 3), arrive_odd(8), arrive_odd(9)],
             odd_edges, odd_sends, edge_low_o, edge_high_o, send_0o, send_3o, mixed_o, start_back)
        new_left(new_lo, (0, 3))
        for c in odd_back:
            c.start()
        for half in range(2):
            value = dot(new_t[...], mixed_o[:, cols(2 * half, 2)]).astype(BF16)
            new_r[cols(2 * half), :] = value[:, 0:D]
            new_r[cols(2 * half + 1), :] = value[:, D : 2 * D]
            hand_over[half].start()
        new_left(new_lo, (1, 2))
        keep_o = pltpu.make_async_copy(new_lo.at[cols(1, 2), :], out.at[1, cols(1, 2), :], local_sem.at[3])
        keep_o.start()
        for c in back + odd_back:
            c.wait_recv()
        for c in back + odd_edges + odd_sends + odd_back + hand_over:
            c.wait_send()
        keep.wait()
        keep_o.wait()

    for c in even_r + edges + sends:
        c.wait_send()


def body(site_tensors, block_counts, gate_even, gate_odd):
    sites = site_tensors.shape[0]
    x = site_tensors.reshape(sites, 4 * D, D)
    hbm = pl.BlockSpec(memory_space=pl.ANY)
    smem = pl.BlockSpec(memory_space=pltpu.SMEM)
    unit = lambda r, c, dtype=BF16: pltpu.VMEM((r * D, c * D), dtype)
    pair = lambda c: pltpu.VMEM((2, D, c * D), BF16)
    phase = [unit(1, 4), unit(1, 3), unit(1, 3), unit(1, 1), unit(1, 1),
             unit(1, 3), unit(1, 3), unit(4, 4)]
    evolved = pl.pallas_call(
        kernel,
        out_shape=jax.ShapeDtypeStruct(x.shape, x.dtype),
        in_specs=[hbm, smem, smem, smem],
        out_specs=hbm,
        scratch_shapes=phase + phase + [
            pltpu.VMEM((2, 4 * D, D), BF16), unit(4, 1), unit(4, 1), unit(4, 1),
            unit(1, 3, F32), unit(2, 4, F32), unit(1, 3, F32),
            unit(3, 4), unit(1, 4), unit(4, 1), unit(4, 1),
            pair(2), pair(1), pair(1), pair(1),
            pltpu.SemaphoreType.DMA((34,)), pltpu.SemaphoreType.DMA((34,)),
            pltpu.SemaphoreType.DMA((4,)), pltpu.SemaphoreType.REGULAR,
        ],
        compiler_params=pltpu.CompilerParams(
            collective_id=0, has_side_effects=True, vmem_limit_bytes=60 * 2**20
        ),
    )(x, block_counts, gate_even, gate_odd)
    return evolved.reshape(site_tensors.shape)


def solution(mesh):
    in_specs = (P("seg", "row", None, None, None), P(), P(), P())
    out_specs = P("seg", "row", None, None, None)
    return jax.shard_map(body, mesh=mesh, in_specs=in_specs, out_specs=out_specs, check_vma=False)
```
